32 devices in a mesh: fsdp: 8 (over z, y), tp: 4 (over x, core).
Axes of the slice: x: 2, y: 2, z: 4, core: 2. Of those that a mesh axis runs over, the one named last changes fastest.
Arguments:
- tokens: bfloat16 [16384, 1024], P(('fsdp', 'tp')), may hold values from -6 to 6
- positions: int32 [16384], P('fsdp'), may hold values from 0 to 3069, as said below
- first_gain: float32 [1024], replicated, may hold values from 0.25 to 1.75
- query_weight: bfloat16 [1024, 1024], P('fsdp', 'tp'), may hold values from -0.1875 to 0.1875
- key_weight: bfloat16 [1024, 512], P('fsdp', 'tp'), may hold values from -0.1875 to 0.1875
- value_weight: bfloat16 [1024, 512], P('fsdp', 'tp'), may hold values from -0.1875 to 0.1875
- query_gain: float32 [64], replicated, may hold values from 0.25 to 1.75
- key_gain: float32 [64], replicated, may hold values from 0.25 to 1.75
- out_weight: bfloat16 [1024, 1024], P('tp', 'fsdp'), may hold values from -2 to 2
- second_gain: float32 [1024], replicated, may hold values from 0.25 to 1.75
- gate_weight: bfloat16 [1024, 4608], P('fsdp', 'tp'), may hold values from -0.1875 to 0.1875
- up_weight: bfloat16 [1024, 4608], P('fsdp', 'tp'), may hold values from -0.1875 to 0.1875
- down_weight: bfloat16 [4608, 1024], P('tp', 'fsdp'), may hold values from -0.09375 to 0.09375
- cotangent: bfloat16 [16384, 1024], P(('fsdp', 'tp')), may hold values from -6 to 6
Outputs:
- output: bfloat16 [16384, 1024], P(('fsdp', 'tp'))
- grad_tokens: float32 [16384, 1024], P(('fsdp', 'tp'))
- grad_first_gain: float32 [1024], replicated
- grad_query_weight: float32 [1024, 1024], P('fsdp', 'tp')
- grad_key_weight: float32 [1024, 512], P('fsdp', 'tp')
- grad_value_weight: float32 [1024, 512], P('fsdp', 'tp')
- grad_query_gain: float32 [64], replicated
- grad_key_gain: float32 [64], replicated
- grad_out_weight: float32 [1024, 1024], P('tp', 'fsdp')
- grad_second_gain: float32 [1024], replicated
- grad_gate_weight: float32 [1024, 4608], P('fsdp', 'tp')
- grad_up_weight: float32 [1024, 4608], P('fsdp', 'tp')
- grad_down_weight: float32 [4608, 1024], P('tp', 'fsdp')
The draws below stay inside these ranges and needn't reach their ends.
Inputs may be any that keep to these rules, and one draw needn't show every extreme that they name: Within each sequence of 1024 consecutive tokens the positions start at 0 and rise by 1 to 3 from each token to the next; in some sequence they rise by 3 at every step.
All inputs are finite; a program needn't handle non-finite values.
Results may differ from the reference program's by a relative error of at most 0.015.
Values may be sent and summed in bfloat16 or wider, within the bound.
A program may use at most 192 MiB of HBM per device.

```python
import math
import jax
import jax.numpy as jnp
from jax import lax

D = 1024
HEADS = 16
KV_HEADS = 8
HEAD_DIM = 64
FF = 4608
SEQ_LEN = 1024
SEQS_GRP = 2
TOKENS = 16384


def draw_positions(key, part):
    key = jax.random.fold_in(key, 11)
    step_key = jax.random.fold_in(key, 1)
    pick_key = jax.random.fold_in(key, 2)
    seq_count = TOKENS // SEQ_LEN
    increments = jax.random.randint(step_key, (seq_count, SEQ_LEN), 1, 4)
    chosen = jax.random.randint(pick_key, (), 0, seq_count)
    steep = (jnp.arange(seq_count) == chosen)[:, None]
    increments = jnp.where(steep, 3, increments)
    starting = (jnp.arange(SEQ_LEN) == 0)[None, :]
    increments = jnp.where(starting, 0, increments)
    return jnp.cumsum(increments, axis=1).reshape(TOKENS).astype(jnp.int32)


def levels(rng, dims, shards, least, largest):
    factor_of = 1.0
    for dim, parts in shards:
        steps = jax.random.uniform(jax.random.fold_in(jax.random.fold_in(rng, 6), dim), (parts,), jnp.float32, least / len(shards), largest / len(shards))
        factor_of = factor_of * jnp.repeat(jnp.exp(steps), dims[dim] // parts).reshape((-1,) + (1,) * (len(dims) - 1 - dim))
    return factor_of


def gaussian(stream_key, dims, deviation, bound, split=(), kind=jnp.bfloat16):
    entries = jax.random.normal(stream_key, dims, jnp.float32) * deviation
    if len(split) > 0:
        entries = levels(stream_key, dims, split, -0.22, 0.18) * entries
    return jnp.clip(entries, min=-bound, max=bound).astype(kind)


def setup_inputs(seed: int = 0) -> dict:
    splits = jax.random.split(jax.random.key(seed), 15)
    return {
        "tokens": gaussian(splits[0], (TOKENS, D), 1.0, 6.0, ((0, 32),)),
        "positions": draw_positions(jax.random.fold_in(splits[14], 71), 0),
        "first_gain": jnp.clip(1.0 + 0.15 * jax.random.normal(splits[2], (D,), jnp.float32), 0.25, 1.75),
        "query_weight": gaussian(splits[3], (D, HEADS * HEAD_DIM), D ** -0.5, 0.1875, ((0, 8), (1, 4))),
        "key_weight": gaussian(splits[4], (D, KV_HEADS * HEAD_DIM), D ** -0.5, 0.1875, ((0, 8), (1, 4))),
        "value_weight": gaussian(splits[5], (D, KV_HEADS * HEAD_DIM), D ** -0.5, 0.1875, ((0, 8), (1, 4))),
        "query_gain": jnp.clip(1.0 + 0.15 * jax.random.normal(splits[6], (HEAD_DIM,), jnp.float32), 0.25, 1.75),
        "key_gain": jnp.clip(1.0 + 0.15 * jax.random.normal(splits[7], (HEAD_DIM,), jnp.float32), 0.25, 1.75),
        "out_weight": gaussian(splits[8], (HEADS * HEAD_DIM, D), (HEADS * HEAD_DIM // 128) ** -0.5, 2.0, ((0, 4), (1, 8))),
        "second_gain": jnp.clip(1.0 + 0.15 * jax.random.normal(splits[9], (D,), jnp.float32), 0.25, 1.75),
        "gate_weight": gaussian(splits[10], (D, FF), D ** -0.5, 0.1875, ((0, 8), (1, 4))),
        "up_weight": gaussian(splits[11], (D, FF), D ** -0.5, 0.1875, ((0, 8), (1, 4))),
        "down_weight": gaussian(splits[12], (FF, D), FF ** -0.5, 0.09375, ((0, 4), (1, 8))),
        "cotangent": gaussian(splits[13], (TOKENS, D), 1.0, 6.0, ((0, 32),)),
    }


EPS = 1e-05
LOG_THETA = math.log(1000000.0)
MASKED = -1e+30
HIGH = lax.Precision.HIGHEST

@jax.custom_vjp
def low(v):
    return lax.optimization_barrier(v.astype(jnp.bfloat16)).astype(jnp.float32)

@jax.custom_vjp
def low_back(v):
    return v

def low_keep(v):
    return (low(v), None)

def low_pass(kept, grad):
    return (grad,)

def back_keep(v):
    return (v, None)

def back_low(kept, grad):
    return (low(grad),)
low.defvjp(low_keep, low_pass)
low_back.defvjp(back_keep, back_low)

def product(left, right):
    return jnp.dot(left, right, preferred_element_type=jnp.float32, precision=HIGH)

def normed(values, gain):
    inverse = lax.rsqrt(lax.optimization_barrier(jnp.mean(values * values, axis=-1, keepdims=True)) + EPS)
    return values * inverse * gain

def angles(positions):
    half_width = HEAD_DIM // 2
    frequency = jnp.exp(-LOG_THETA * 2.0 * jnp.arange(half_width, dtype=jnp.float32) / HEAD_DIM)
    rotation = positions.astype(jnp.float32)[:, None] * frequency[None, :]
    return (jnp.cos(rotation)[:, None, :], jnp.sin(rotation)[:, None, :])

def rotate(values, cosine, sine):
    half_width = HEAD_DIM // 2
    first_half = values[..., :half_width]
    second_half = values[..., half_width:]
    return jnp.concatenate([first_half * cosine - second_half * sine, second_half * cosine + first_half * sine], axis=-1)

def attend(sequence_items):
    query_rot, key_rot, value_rot = sequence_items
    repeat_count = HEADS // KV_HEADS
    key_rows = jnp.repeat(key_rot, repeat_count, axis=1)
    value_rows = jnp.repeat(value_rot, repeat_count, axis=1)
    scores = jnp.einsum('ihd,jhd->hij', query_rot, key_rows, precision=HIGH) * HEAD_DIM ** (-0.5)
    scores = low_back(scores)
    row_ids = jnp.arange(SEQ_LEN)
    allowed = row_ids[:, None] >= row_ids[None, :]
    scores = jnp.where(allowed[None], scores, MASKED)
    softmax_prob = jax.nn.softmax(scores, axis=-1)
    context = jnp.einsum('hij,jhd->ihd', low(softmax_prob), value_rows, precision=HIGH)
    return context.reshape(SEQ_LEN, HEADS * HEAD_DIM)

def reference(tokens, positions, first_gain, query_weight, key_weight, value_weight, query_gain, key_gain, out_weight, second_gain, gate_weight, up_weight, down_weight, cotangent):
    group_rows = SEQS_GRP * SEQ_LEN
    group_count = TOKENS // group_rows
    cosine, sine = angles(positions)
    cosine = cosine.reshape(group_count, group_rows, 1, HEAD_DIM // 2)
    sine = sine.reshape(group_count, group_rows, 1, HEAD_DIM // 2)

    def forward(inputs, gain_one, w_query, w_key, w_value, gain_query, gain_key, w_out, gain_two, w_gate, w_up, w_down):

        def one_group(group_items):
            rows, cos_rows, sin_rows = group_items
            normed_one = low(normed(rows, gain_one))
            query_proj = low_back(product(normed_one, w_query)).reshape(group_rows, HEADS, HEAD_DIM)
            key_proj = low_back(product(normed_one, w_key)).reshape(group_rows, KV_HEADS, HEAD_DIM)
            value_proj = low(low_back(product(normed_one, w_value))).reshape(group_rows, KV_HEADS, HEAD_DIM)
            query_rot = low(rotate(normed(query_proj, gain_query), cos_rows, sin_rows))
            key_rot = low(rotate(normed(key_proj, gain_key), cos_rows, sin_rows))
            context = lax.map(jax.checkpoint(attend), (query_rot.reshape(SEQS_GRP, SEQ_LEN, HEADS, HEAD_DIM), key_rot.reshape(SEQS_GRP, SEQ_LEN, KV_HEADS, HEAD_DIM), value_proj.reshape(SEQS_GRP, SEQ_LEN, KV_HEADS, HEAD_DIM)))
            context = low(low_back(context.reshape(group_rows, HEADS * HEAD_DIM)))
            hidden = rows + low_back(product(context, w_out))
            normed_two = low(normed(hidden, gain_two))
            gate_value = low_back(product(normed_two, w_gate))
            up_value = low_back(product(normed_two, w_up))
            mixed_units = low(jax.nn.silu(gate_value) * up_value)
            return hidden + product(mixed_units, w_down)
        stacked = lax.map(jax.checkpoint(one_group), (inputs.reshape(group_count, group_rows, D), cosine, sine))
        return stacked.reshape(TOKENS, D)
    result, pull = jax.vjp(forward, tokens.astype(jnp.float32), first_gain.astype(jnp.float32), query_weight.astype(jnp.float32), key_weight.astype(jnp.float32), value_weight.astype(jnp.float32), query_gain.astype(jnp.float32), key_gain.astype(jnp.float32), out_weight.astype(jnp.float32), second_gain.astype(jnp.float32), gate_weight.astype(jnp.float32), up_weight.astype(jnp.float32), down_weight.astype(jnp.float32))
    grads = pull(cotangent.astype(jnp.float32))
    return (result.astype(jnp.bfloat16), grads[0], grads[1], grads[2], grads[3], grads[4], grads[5], grads[6], grads[7], grads[8], grads[9], grads[10], grads[11])
```

```python
import functools
import math

import jax
import jax.numpy as jnp
from jax import lax
from jax.experimental import pallas as pl
from jax.experimental.pallas import tpu as pltpu
from jax.sharding import PartitionSpec as P

HEAD_DIM = 64
SEQ_LEN = 1024


EPS = 1e-05
LOG_THETA = math.log(1000000.0)
MASKED = -1e30


def dot_plain(left, right):
    return jnp.dot(left, right, preferred_element_type=jnp.float32)


def dot_rows(left, right):
    return lax.dot_general(
        left, right, (((0,), (0,)), ((), ())), preferred_element_type=jnp.float32
    )


def dot_cols(left, right):
    return lax.dot_general(
        left, right, (((1,), (1,)), ((), ())), preferred_element_type=jnp.float32
    )


def normalize(values):
    inverse = lax.rsqrt(jnp.mean(values * values, axis=-1, keepdims=True) + EPS)
    return (values * inverse, inverse)


def norm_back(grad_unit, unit_values, inverse):
    return inverse * (
        grad_unit - unit_values * jnp.mean(grad_unit * unit_values, axis=-1, keepdims=True)
    )


def angle_tables(positions):
    half_width = HEAD_DIM // 2
    frequency = jnp.exp(-LOG_THETA * 2.0 * jnp.arange(half_width, dtype=jnp.float32) / HEAD_DIM)
    rotation = positions.astype(jnp.float32)[None, :] * frequency[:, None]
    cosine, sine = jnp.cos(rotation), jnp.sin(rotation)
    cosine_table = jnp.concatenate([cosine, cosine, cosine, cosine], axis=0).T
    sine_table = jnp.concatenate([-sine, sine, -sine, sine], axis=0).T
    return (cosine_table, sine_table)


def widen(table, width):
    return jnp.concatenate([table] * (width // table.shape[1]), axis=1)


def swap_halves(values):
    width = values.shape[1]
    half_width = HEAD_DIM // 2
    lane = lax.broadcasted_iota(jnp.int32, values.shape, 1)
    ahead = pltpu.roll(values, width - half_width, 1)
    behind = pltpu.roll(values, half_width, 1)
    return jnp.where(lane % HEAD_DIM < half_width, ahead, behind)


def head_mean(values):
    width = values.shape[1]
    row_head = lax.broadcasted_iota(jnp.int32, (width, width), 0) // HEAD_DIM
    col_head = lax.broadcasted_iota(jnp.int32, (width, width), 1) // HEAD_DIM
    spread = jnp.where(row_head == col_head, 1.0 / HEAD_DIM, 0.0).astype(jnp.float32)
    return jnp.dot(
        values, spread, preferred_element_type=jnp.float32, precision=lax.Precision.HIGHEST
    )


def head_units(values):
    inverse = lax.rsqrt(head_mean(values * values) + EPS)
    return (values * inverse, inverse)


def masked_scores(key_rows, query_rows, first_row, block_rows):
    scores = dot_cols(key_rows, query_rows)
    key_index = lax.broadcasted_iota(jnp.int32, scores.shape, 0)
    row_index = first_row + lax.broadcasted_iota(jnp.int32, scores.shape, 1) % block_rows
    return jnp.where(key_index <= row_index, scores, MASKED)


def stacked_heads(ref, first_row, block_rows, pair, share):
    return jnp.concatenate(
        [
            ref[
                first_row : first_row + block_rows,
                (pair * share + member) * HEAD_DIM : (pair * share + member + 1) * HEAD_DIM,
            ]
            for member in range(share)
        ],
        axis=0,
    )


def forward_kernel(
    pairs, share, block_rows, proj_ref, cosine_ref, sine_ref, query_gain_ref, key_gain_ref,
    rot_ref, context_ref, logsum_ref,
):
    length = proj_ref.shape[0]
    query_width = pairs * share * HEAD_DIM
    key_width = pairs * HEAD_DIM
    cosine, sine = cosine_ref[...], sine_ref[...]
    query_unit, _ = head_units(proj_ref[:, :query_width])
    key_unit, _ = head_units(proj_ref[:, query_width : query_width + key_width])
    query_scaled = query_unit * query_gain_ref[...]
    key_scaled = key_unit * key_gain_ref[...]
    rot_ref[:, :query_width] = (
        query_scaled * widen(cosine, query_width)
        + swap_halves(query_scaled) * widen(sine, query_width)
    ).astype(jnp.bfloat16)
    rot_ref[:, query_width : query_width + key_width] = (
        key_scaled * widen(cosine, key_width) + swap_halves(key_scaled) * widen(sine, key_width)
    ).astype(jnp.bfloat16)
    rot_ref[:, query_width + key_width :] = proj_ref[:, query_width + key_width :].astype(
        jnp.bfloat16
    )
    for pair in range(pairs):
        key_lanes = slice(query_width + pair * HEAD_DIM, query_width + (pair + 1) * HEAD_DIM)
        value_lanes = slice(key_lanes.start + key_width, key_lanes.stop + key_width)
        for first_row in range(0, length, block_rows):
            last_row = first_row + block_rows
            query_rows = stacked_heads(rot_ref, first_row, block_rows, pair, share)
            query_rows = query_rows * jnp.asarray(HEAD_DIM ** (-0.5), jnp.bfloat16)
            scores = masked_scores(
                rot_ref[:last_row, key_lanes], query_rows, first_row, block_rows
            )
            weights = jnp.exp(scores)
            total = jnp.sum(weights, axis=0, keepdims=True)
            context = dot_rows(rot_ref[:last_row, value_lanes], weights.astype(jnp.bfloat16))
            context = (context / total).T.astype(jnp.bfloat16)
            logsum = jnp.log(total)
            for member in range(share):
                head = pair * share + member
                here = slice(member * block_rows, (member + 1) * block_rows)
                context_ref[
                    first_row:last_row, head * HEAD_DIM : (head + 1) * HEAD_DIM
                ] = context[here]
                logsum_ref[head : head + 1, first_row:last_row] = logsum[:, here]


def backward_kernel(
    pairs, share, block_rows, proj_ref, cosine_ref, sine_ref, query_gain_ref, key_gain_ref,
    rot_ref, logsum_ref, grad_context_ref,
    grad_proj_ref, gain_sum_ref, query_total, key_total, value_total,
):
    length = proj_ref.shape[0]
    query_width = pairs * share * HEAD_DIM
    key_width = pairs * HEAD_DIM
    scale = HEAD_DIM ** (-0.5)
    for pair in range(pairs):
        key_lanes = slice(query_width + pair * HEAD_DIM, query_width + (pair + 1) * HEAD_DIM)
        value_lanes = slice(key_lanes.start + key_width, key_lanes.stop + key_width)
        pair_lanes = slice(pair * HEAD_DIM, (pair + 1) * HEAD_DIM)
        for first_row in reversed(range(0, length, block_rows)):
            last_row = first_row + block_rows
            query_rows = stacked_heads(rot_ref, first_row, block_rows, pair, share)
            query_rows = query_rows * jnp.asarray(scale, jnp.bfloat16)
            grad_rows = stacked_heads(grad_context_ref, first_row, block_rows, pair, share)
            logsum = jnp.concatenate(
                [
                    logsum_ref[pair * share + member : pair * share + member + 1, first_row:last_row]
                    for member in range(share)
                ],
                axis=1,
            )
            key_rows = rot_ref[:last_row, key_lanes]
            scores = masked_scores(key_rows, query_rows, first_row, block_rows)
            prob = jnp.exp(scores - logsum)
            grad_prob = dot_cols(rot_ref[:last_row, value_lanes], grad_rows)
            inner = jnp.sum(prob * grad_prob, axis=0, keepdims=True)
            grad_score = (prob * (grad_prob - inner)).astype(jnp.bfloat16)
            grad_query = (dot_rows(key_rows, grad_score) * scale).T
            for member in range(share):
                head = pair * share + member
                query_total[
                    first_row:last_row, head * HEAD_DIM : (head + 1) * HEAD_DIM
                ] = grad_query[member * block_rows : (member + 1) * block_rows]
            grad_key = dot_plain(grad_score, query_rows)
            grad_value = dot_plain(prob.astype(jnp.bfloat16), grad_rows)
            if last_row == length:
                key_total[:, pair_lanes] = grad_key
                value_total[:, pair_lanes] = grad_value
            else:
                key_total[:last_row, pair_lanes] += grad_key
                value_total[:last_row, pair_lanes] += grad_value
    cosine, sine = cosine_ref[...], sine_ref[...]
    for lanes, total, gain_ref in (
        (slice(0, query_width), query_total, query_gain_ref),
        (slice(query_width, query_width + key_width), key_total, key_gain_ref),
    ):
        width = lanes.stop - lanes.start
        unit, inverse = head_units(proj_ref[:, lanes])
        grads = total[...]
        grad_normed = grads * widen(cosine, width) - swap_halves(grads) * widen(sine, width)
        gain_sum_ref[0:1, lanes] = jnp.sum(grad_normed * unit, axis=0, keepdims=True)
        scaled = grad_normed * gain_ref[...]
        grad_proj_ref[:, lanes] = (
            inverse * (scaled - unit * head_mean(scaled * unit))
        ).astype(jnp.bfloat16)
    grad_proj_ref[:, query_width + key_width :] = value_total[...].astype(jnp.bfloat16)


def row_spec(width):
    return pl.BlockSpec((SEQ_LEN, width), lambda sequence: (sequence, 0))


def whole_spec(width):
    return pl.BlockSpec((1, width), lambda sequence: (0, 0))


def attention_forward(proj, tables, gain_rows, pairs, share):
    rows, width = proj.shape
    query_width = pairs * share * HEAD_DIM
    key_width = pairs * HEAD_DIM
    sequences = rows // SEQ_LEN
    return pl.pallas_call(
        functools.partial(forward_kernel, pairs, share, min(256, SEQ_LEN)),
        grid=(sequences,),
        in_specs=[
            row_spec(width), row_spec(128), row_spec(128),
            whole_spec(query_width), whole_spec(key_width),
        ],
        out_specs=[
            row_spec(width),
            row_spec(query_width),
            pl.BlockSpec((8, SEQ_LEN), lambda sequence: (sequence, 0)),
        ],
        out_shape=[
            jax.ShapeDtypeStruct((rows, width), jnp.bfloat16),
            jax.ShapeDtypeStruct((rows, query_width), jnp.bfloat16),
            jax.ShapeDtypeStruct((sequences * 8, SEQ_LEN), jnp.float32),
        ],
        compiler_params=pltpu.CompilerParams(vmem_limit_bytes=48 * 1024 * 1024),
        cost_estimate=pl.CostEstimate(
            flops=4 * rows * SEQ_LEN * query_width,
            bytes_accessed=10 * rows * width,
            transcendentals=rows * SEQ_LEN * pairs * share,
        ),
        name="attention_forward",
    )(proj, *tables, *gain_rows)


def attention_backward(proj, tables, gain_rows, rot, logsums, grad_context, pairs, share):
    rows, width = proj.shape
    query_width = pairs * share * HEAD_DIM
    key_width = pairs * HEAD_DIM
    sequences = rows // SEQ_LEN
    return pl.pallas_call(
        functools.partial(backward_kernel, pairs, share, min(256, SEQ_LEN)),
        grid=(sequences,),
        in_specs=[
            row_spec(width), row_spec(128), row_spec(128),
            whole_spec(query_width), whole_spec(key_width),
            row_spec(width),
            pl.BlockSpec((8, SEQ_LEN), lambda sequence: (sequence, 0)),
            row_spec(query_width),
        ],
        out_specs=[
            row_spec(width),
            pl.BlockSpec((8, query_width + key_width), lambda sequence: (sequence, 0)),
        ],
        out_shape=[
            jax.ShapeDtypeStruct((rows, width), jnp.bfloat16),
            jax.ShapeDtypeStruct((sequences * 8, query_width + key_width), jnp.float32),
        ],
        scratch_shapes=[
            pltpu.VMEM((SEQ_LEN, query_width), jnp.float32),
            pltpu.VMEM((SEQ_LEN, key_width), jnp.float32),
            pltpu.VMEM((SEQ_LEN, key_width), jnp.float32),
        ],
        compiler_params=pltpu.CompilerParams(vmem_limit_bytes=48 * 1024 * 1024),
        cost_estimate=pl.CostEstimate(
            flops=10 * rows * SEQ_LEN * query_width,
            bytes_accessed=14 * rows * width,
            transcendentals=rows * SEQ_LEN * pairs * share,
        ),
        name="attention_backward",
    )(proj, *tables, *gain_rows, rot, logsums, grad_context)


def gather_tokens(rows):
    return lax.all_gather(rows, "tp", axis=0, tiled=True)


def scatter_tokens(partial):
    return lax.psum_scatter(
        partial.astype(jnp.bfloat16), "tp", scatter_dimension=0, tiled=True
    ).astype(jnp.float32)


def on_device(
    tokens,
    positions,
    first_gain,
    query_weight,
    key_weight,
    value_weight,
    query_gain,
    key_gain,
    out_weight,
    second_gain,
    gate_weight,
    up_weight,
    down_weight,
    cotangent,
):
    group_rows = positions.shape[0]
    heads_here = query_weight.shape[1] // HEAD_DIM
    pairs_here = key_weight.shape[1] // HEAD_DIM
    share = heads_here // pairs_here
    query_width = query_weight.shape[1]
    key_width = key_weight.shape[1]
    proj_width = query_width + 2 * key_width
    units = gate_weight.shape[1]
    attention_weights = lax.all_gather(
        jnp.concatenate([query_weight, key_weight, value_weight, out_weight.T], axis=1),
        "fsdp", axis=0, tiled=True,
    )
    unit_weights = lax.all_gather(
        jnp.concatenate([gate_weight, up_weight, down_weight.T], axis=1),
        "fsdp", axis=0, tiled=True,
    )
    whole_proj = attention_weights[:, :proj_width]
    whole_out = attention_weights[:, proj_width:]
    whole_gate = unit_weights[:, :units]
    whole_up = unit_weights[:, units : 2 * units]
    whole_down = unit_weights[:, 2 * units :]
    inputs = tokens.astype(jnp.float32)
    unit_one, inverse_one = normalize(inputs)
    normed_one = gather_tokens((unit_one * first_gain).astype(jnp.bfloat16))
    proj = dot_plain(normed_one, whole_proj)
    tables = angle_tables(positions)
    gain_rows = (
        jnp.tile(query_gain, heads_here)[None, :], jnp.tile(key_gain, pairs_here)[None, :]
    )
    rot, context, logsums = attention_forward(proj, tables, gain_rows, pairs_here, share)
    hidden = inputs + scatter_tokens(dot_cols(context, whole_out))
    unit_two, inverse_two = normalize(hidden)
    normed_two = gather_tokens((unit_two * second_gain).astype(jnp.bfloat16))
    grad_result = gather_tokens(cotangent)
    gate_value = dot_plain(normed_two, whole_gate)
    up_value = dot_plain(normed_two, whole_up)
    sigmoid_gate = jax.nn.sigmoid(gate_value)
    active = gate_value * sigmoid_gate
    mixed_units = (active * up_value).astype(jnp.bfloat16)
    grad_mixed = dot_plain(grad_result, whole_down)
    grad_gate = (
        grad_mixed * up_value * sigmoid_gate * (1.0 + gate_value * (1.0 - sigmoid_gate))
    ).astype(jnp.bfloat16)
    grad_up = (grad_mixed * active).astype(jnp.bfloat16)
    grad_normed_two = scatter_tokens(
        dot_cols(grad_gate, whole_gate) + dot_cols(grad_up, whole_up)
    )
    result = hidden + scatter_tokens(dot_cols(mixed_units, whole_down))
    output = result.astype(jnp.bfloat16)
    unit_grads = jnp.concatenate(
        [
            dot_rows(normed_two, grad_gate).astype(jnp.bfloat16),
            dot_rows(normed_two, grad_up).astype(jnp.bfloat16),
            dot_rows(grad_result, mixed_units).astype(jnp.bfloat16),
        ],
        axis=1,
    )
    grad_normed_two, unit_grads = lax.optimization_barrier((grad_normed_two, unit_grads))
    unit_shard = lax.psum_scatter(unit_grads, "fsdp", scatter_dimension=0, tiled=True)
    gain_two = jnp.sum(grad_normed_two * unit_two, axis=0)
    grad_hidden = cotangent.astype(jnp.float32) + norm_back(
        grad_normed_two * second_gain, unit_two, inverse_two
    )
    grad_hidden_all = gather_tokens(grad_hidden.astype(jnp.bfloat16))
    grad_context = dot_plain(grad_hidden_all, whole_out).astype(jnp.bfloat16)
    grad_proj, gain_sums = attention_backward(
        proj, tables, gain_rows, rot, logsums, grad_context, pairs_here, share
    )
    grad_normed_one = scatter_tokens(dot_cols(grad_proj, whole_proj))
    attention_grads = jnp.concatenate(
        [
            dot_rows(normed_one, grad_proj).astype(jnp.bfloat16),
            dot_rows(grad_hidden_all, context).astype(jnp.bfloat16),
        ],
        axis=1,
    )
    attention_shard = lax.psum_scatter(
        attention_grads, "fsdp", scatter_dimension=0, tiled=True
    ).astype(jnp.float32)
    gain_one = jnp.sum(grad_normed_one * unit_one, axis=0)
    grad_tokens = grad_hidden + norm_back(grad_normed_one * first_gain, unit_one, inverse_one)
    gain_sums = jnp.sum(gain_sums.reshape(-1, 8, query_width + key_width)[:, 0], axis=0)
    gain_query = jnp.sum(gain_sums[:query_width].reshape(heads_here, HEAD_DIM), axis=0)
    gain_key = jnp.sum(gain_sums[query_width:].reshape(pairs_here, HEAD_DIM), axis=0)
    width = first_gain.shape[0]
    gains = lax.psum(
        jnp.concatenate([gain_one, gain_two, gain_query, gain_key]), ("fsdp", "tp")
    )
    unit_shard = unit_shard.astype(jnp.float32)
    return (
        output,
        grad_tokens,
        gains[:width],
        attention_shard[:, :query_width],
        attention_shard[:, query_width : query_width + key_width],
        attention_shard[:, query_width + key_width : proj_width],
        gains[2 * width : 2 * width + HEAD_DIM],
        gains[2 * width + HEAD_DIM :],
        attention_shard[:, proj_width:].T,
        gains[width : 2 * width],
        unit_shard[:, :units],
        unit_shard[:, units : 2 * units],
        unit_shard[:, 2 * units :].T,
    )


def solution(mesh):
    return jax.shard_map(
        on_device,
        mesh=mesh,
        in_specs=(
            P(("fsdp", "tp"), None),
            P("fsdp"),
            P(),
            P("fsdp", "tp"),
            P("fsdp", "tp"),
            P("fsdp", "tp"),
            P(),
            P(),
            P("tp", "fsdp"),
            P(),
            P("fsdp", "tp"),
            P("fsdp", "tp"),
            P("tp", "fsdp"),
            P(("fsdp", "tp"), None),
        ),
        out_specs=(
            P(("fsdp", "tp"), None),
            P(("fsdp", "tp"), None),
            P(),
            P("fsdp", "tp"),
            P("fsdp", "tp"),
            P("fsdp", "tp"),
            P(),
            P(),
            P("tp", "fsdp"),
            P(),
            P("fsdp", "tp"),
            P("fsdp", "tp"),
            P("tp", "fsdp"),
        ),
        check_vma=False,
    )
```

```python
import functools
import math

import jax
import jax.numpy as jnp
from jax import lax
from jax.experimental import pallas as pl
from jax.experimental.pallas import tpu as pltpu
from jax.sharding import PartitionSpec as P

HEAD_DIM = 64
SEQ_LEN = 1024


EPS = 1e-05
LOG_THETA = math.log(1000000.0)
MASKED = -1e30


def dot_plain(left, right):
    return jnp.dot(left, right, preferred_element_type=jnp.float32)


def dot_rows(left, right):
    return lax.dot_general(
        left, right, (((0,), (0,)), ((), ())), preferred_element_type=jnp.float32
    )


def dot_cols(left, right):
    return lax.dot_general(
        left, right, (((1,), (1,)), ((), ())), preferred_element_type=jnp.float32
    )


def normalize(values):
    inverse = lax.rsqrt(jnp.mean(values * values, axis=-1, keepdims=True) + EPS)
    return (values * inverse, inverse)


def norm_back(grad_unit, unit_values, inverse):
    return inverse * (
        grad_unit - unit_values * jnp.mean(grad_unit * unit_values, axis=-1, keepdims=True)
    )


def angle_tables(positions):
    half_width = HEAD_DIM // 2
    frequency = jnp.exp(-LOG_THETA * 2.0 * jnp.arange(half_width, dtype=jnp.float32) / HEAD_DIM)
    rotation = positions.astype(jnp.float32)[None, :] * frequency[:, None]
    cosine, sine = jnp.cos(rotation), jnp.sin(rotation)
    cosine_table = jnp.concatenate([cosine, cosine, cosine, cosine], axis=0).T
    sine_table = jnp.concatenate([-sine, sine, -sine, sine], axis=0).T
    return (cosine_table, sine_table)


def widen(table, width):
    return jnp.concatenate([table] * (width // table.shape[1]), axis=1)


def swap_halves(values):
    width = values.shape[1]
    half_width = HEAD_DIM // 2
    lane = lax.broadcasted_iota(jnp.int32, values.shape, 1)
    ahead = pltpu.roll(values, width - half_width, 1)
    behind = pltpu.roll(values, half_width, 1)
    return jnp.where(lane % HEAD_DIM < half_width, ahead, behind)


def head_mean(values):
    width = values.shape[1]
    row_head = lax.broadcasted_iota(jnp.int32, (width, width), 0) // HEAD_DIM
    col_head = lax.broadcasted_iota(jnp.int32, (width, width), 1) // HEAD_DIM
    spread = jnp.where(row_head == col_head, 1.0 / HEAD_DIM, 0.0).astype(jnp.float32)
    return jnp.dot(
        values, spread, preferred_element_type=jnp.float32, precision=lax.Precision.HIGHEST
    )


def head_units(values):
    inverse = lax.rsqrt(head_mean(values * values) + EPS)
    return (values * inverse, inverse)


def masked_scores(key_rows, query_rows, first_row, block_rows):
    scores = dot_cols(key_rows, query_rows)
    key_index = lax.broadcasted_iota(jnp.int32, scores.shape, 0)
    row_index = first_row + lax.broadcasted_iota(jnp.int32, scores.shape, 1) % block_rows
    return jnp.where(key_index <= row_index, scores, MASKED)


def stacked_heads(ref, first_row, block_rows, pair, share):
    return jnp.concatenate(
        [
            ref[
                first_row : first_row + block_rows,
                (pair * share + member) * HEAD_DIM : (pair * share + member + 1) * HEAD_DIM,
            ]
            for member in range(share)
        ],
        axis=0,
    )


def forward_kernel(
    pairs, share, block_rows, proj_ref, cosine_ref, sine_ref, query_gain_ref, key_gain_ref,
    rot_ref, context_ref, logsum_ref,
):
    length = proj_ref.shape[0]
    query_width = pairs * share * HEAD_DIM
    key_width = pairs * HEAD_DIM
    cosine, sine = cosine_ref[...], sine_ref[...]
    query_unit, _ = head_units(proj_ref[:, :query_width])
    key_unit, _ = head_units(proj_ref[:, query_width : query_width + key_width])
    query_scaled = query_unit * query_gain_ref[...]
    key_scaled = key_unit * key_gain_ref[...]
    rot_ref[:, :query_width] = (
        query_scaled * widen(cosine, query_width)
        + swap_halves(query_scaled) * widen(sine, query_width)
    ).astype(jnp.bfloat16)
    rot_ref[:, query_width : query_width + key_width] = (
        key_scaled * widen(cosine, key_width) + swap_halves(key_scaled) * widen(sine, key_width)
    ).astype(jnp.bfloat16)
    rot_ref[:, query_width + key_width :] = proj_ref[:, query_width + key_width :].astype(
        jnp.bfloat16
    )
    for pair in range(pairs):
        key_lanes = slice(query_width + pair * HEAD_DIM, query_width + (pair + 1) * HEAD_DIM)
        value_lanes = slice(key_lanes.start + key_width, key_lanes.stop + key_width)
        for first_row in range(0, length, block_rows):
            last_row = first_row + block_rows
            query_rows = stacked_heads(rot_ref, first_row, block_rows, pair, share)
            query_rows = query_rows * jnp.asarray(HEAD_DIM ** (-0.5), jnp.bfloat16)
            scores = masked_scores(
                rot_ref[:last_row, key_lanes], query_rows, first_row, block_rows
            )
            weights = jnp.exp(scores)
            total = jnp.sum(weights, axis=0, keepdims=True)
            context = dot_rows(rot_ref[:last_row, value_lanes], weights.astype(jnp.bfloat16))
            context = (context / total).T.astype(jnp.bfloat16)
            logsum = jnp.log(total)
            for member in range(share):
                head = pair * share + member
                here = slice(member * block_rows, (member + 1) * block_rows)
                context_ref[
                    first_row:last_row, head * HEAD_DIM : (head + 1) * HEAD_DIM
                ] = context[here]
                logsum_ref[head : head + 1, first_row:last_row] = logsum[:, here]


def backward_kernel(
    pairs, share, block_rows, proj_ref, cosine_ref, sine_ref, query_gain_ref, key_gain_ref,
    rot_ref, logsum_ref, grad_context_ref,
    grad_proj_ref, gain_sum_ref, query_total, key_total, value_total,
):
    length = proj_ref.shape[0]
    query_width = pairs * share * HEAD_DIM
    key_width = pairs * HEAD_DIM
    scale = HEAD_DIM ** (-0.5)
    for pair in range(pairs):
        key_lanes = slice(query_width + pair * HEAD_DIM, query_width + (pair + 1) * HEAD_DIM)
        value_lanes = slice(key_lanes.start + key_width, key_lanes.stop + key_width)
        pair_lanes = slice(pair * HEAD_DIM, (pair + 1) * HEAD_DIM)
        for first_row in reversed(range(0, length, block_rows)):
            last_row = first_row + block_rows
            query_rows = stacked_heads(rot_ref, first_row, block_rows, pair, share)
            query_rows = query_rows * jnp.asarray(scale, jnp.bfloat16)
            grad_rows = stacked_heads(grad_context_ref, first_row, block_rows, pair, share)
            logsum = jnp.concatenate(
                [
                    logsum_ref[pair * share + member : pair * share + member + 1, first_row:last_row]
                    for member in range(share)
                ],
                axis=1,
            )
            key_rows = rot_ref[:last_row, key_lanes]
            scores = masked_scores(key_rows, query_rows, first_row, block_rows)
            prob = jnp.exp(scores - logsum)
            grad_prob = dot_cols(rot_ref[:last_row, value_lanes], grad_rows)
            inner = jnp.sum(prob * grad_prob, axis=0, keepdims=True)
            grad_score = (prob * (grad_prob - inner)).astype(jnp.bfloat16)
            grad_query = (dot_rows(key_rows, grad_score) * scale).T
            for member in range(share):
                head = pair * share + member
                query_total[
                    first_row:last_row, head * HEAD_DIM : (head + 1) * HEAD_DIM
                ] = grad_query[member * block_rows : (member + 1) * block_rows]
            grad_key = dot_plain(grad_score, query_rows)
            grad_value = dot_plain(prob.astype(jnp.bfloat16), grad_rows)
            if last_row == length:
                key_total[:, pair_lanes] = grad_key
                value_total[:, pair_lanes] = grad_value
            else:
                key_total[:last_row, pair_lanes] += grad_key
                value_total[:last_row, pair_lanes] += grad_value
    cosine, sine = cosine_ref[...], sine_ref[...]
    for lanes, total, gain_ref in (
        (slice(0, query_width), query_total, query_gain_ref),
        (slice(query_width, query_width + key_width), key_total, key_gain_ref),
    ):
        width = lanes.stop - lanes.start
        unit, inverse = head_units(proj_ref[:, lanes])
        grads = total[...]
        grad_normed = grads * widen(cosine, width) - swap_halves(grads) * widen(sine, width)
        gain_sum_ref[0:1, lanes] = jnp.sum(grad_normed * unit, axis=0, keepdims=True)
        scaled = grad_normed * gain_ref[...]
        grad_proj_ref[:, lanes] = (
            inverse * (scaled - unit * head_mean(scaled * unit))
        ).astype(jnp.bfloat16)
    grad_proj_ref[:, query_width + key_width :] = value_total[...].astype(jnp.bfloat16)


def row_spec(width):
    return pl.BlockSpec((SEQ_LEN, width), lambda sequence: (sequence, 0))


def whole_spec(width):
    return pl.BlockSpec((1, width), lambda sequence: (0, 0))


def attention_forward(proj, tables, gain_rows, pairs, share):
    rows, width = proj.shape
    query_width = pairs * share * HEAD_DIM
    key_width = pairs * HEAD_DIM
    sequences = rows // SEQ_LEN
    return pl.pallas_call(
        functools.partial(forward_kernel, pairs, share, min(256, SEQ_LEN)),
        grid=(sequences,),
        in_specs=[
            row_spec(width), row_spec(128), row_spec(128),
            whole_spec(query_width), whole_spec(key_width),
        ],
        out_specs=[
            row_spec(width),
            row_spec(query_width),
            pl.BlockSpec((8, SEQ_LEN), lambda sequence: (sequence, 0)),
        ],
        out_shape=[
            jax.ShapeDtypeStruct((rows, width), jnp.bfloat16),
            jax.ShapeDtypeStruct((rows, query_width), jnp.bfloat16),
            jax.ShapeDtypeStruct((sequences * 8, SEQ_LEN), jnp.float32),
        ],
        compiler_params=pltpu.CompilerParams(vmem_limit_bytes=48 * 1024 * 1024),
        cost_estimate=pl.CostEstimate(
            flops=4 * rows * SEQ_LEN * query_width,
            bytes_accessed=10 * rows * width,
            transcendentals=rows * SEQ_LEN * pairs * share,
        ),
        name="attention_forward",
    )(proj, *tables, *gain_rows)


def attention_backward(proj, tables, gain_rows, rot, logsums, grad_context, pairs, share):
    rows, width = proj.shape
    query_width = pairs * share * HEAD_DIM
    key_width = pairs * HEAD_DIM
    sequences = rows // SEQ_LEN
    return pl.pallas_call(
        functools.partial(backward_kernel, pairs, share, min(256, SEQ_LEN)),
        grid=(sequences,),
        in_specs=[
            row_spec(width), row_spec(128), row_spec(128),
            whole_spec(query_width), whole_spec(key_width),
            row_spec(width),
            pl.BlockSpec((8, SEQ_LEN), lambda sequence: (sequence, 0)),
            row_spec(query_width),
        ],
        out_specs=[
            row_spec(width),
            pl.BlockSpec((8, query_width + key_width), lambda sequence: (sequence, 0)),
        ],
        out_shape=[
            jax.ShapeDtypeStruct((rows, width), jnp.bfloat16),
            jax.ShapeDtypeStruct((sequences * 8, query_width + key_width), jnp.float32),
        ],
        scratch_shapes=[
            pltpu.VMEM((SEQ_LEN, query_width), jnp.float32),
            pltpu.VMEM((SEQ_LEN, key_width), jnp.float32),
            pltpu.VMEM((SEQ_LEN, key_width), jnp.float32),
        ],
        compiler_params=pltpu.CompilerParams(vmem_limit_bytes=48 * 1024 * 1024),
        cost_estimate=pl.CostEstimate(
            flops=2 * rows * width,
            bytes_accessed=rows * width,
            transcendentals=0,
        ),
        name="attention_backward",
    )(proj, *tables, *gain_rows, rot, logsums, grad_context)


MESH_ID = pl.DeviceIdType.MESH
CHUNKS = 4


def greet(peers):
    barrier = pltpu.get_barrier_semaphore()
    for peer in peers:
        pl.semaphore_signal(barrier, inc=1, device_id=peer, device_id_type=MESH_ID)
    pl.semaphore_wait(barrier, len(peers))


def tp_partners():
    me = lax.axis_index("tp")
    near = me + 1 - 2 * lax.rem(me, 2)
    far = lax.rem(me + 2, 4)
    return (me, near, far)


def gather_kernel(
    rows_ref, whole_ref, local_sem, near_send, near_recv, far_send, far_recv, pass_send, pass_recv
):
    me, near, far = tp_partners()
    rows = rows_ref.shape[0]
    step = rows // CHUNKS

    def remote(source, target, sends, recvs, chunk, peer):
        return pltpu.make_async_remote_copy(
            src_ref=source, dst_ref=target, send_sem=sends.at[chunk], recv_sem=recvs.at[chunk],
            device_id={"tp": peer}, device_id_type=MESH_ID,
        )

    greet([{"tp": near}, {"tp": far}])
    far_copies = []
    near_copies = []
    for chunk in range(CHUNKS):
        source = rows_ref.at[pl.ds(chunk * step, step)]
        target = whole_ref.at[pl.ds(pl.multiple_of(me * rows + chunk * step, step), step)]
        far_copies.append(remote(source, target, far_send, far_recv, chunk, far))
        far_copies[-1].start()
    for chunk in range(CHUNKS):
        source = rows_ref.at[pl.ds(chunk * step, step)]
        target = whole_ref.at[pl.ds(pl.multiple_of(me * rows + chunk * step, step), step)]
        near_copies.append(remote(source, target, near_send, near_recv, chunk, near))
        near_copies[-1].start()
    local = pltpu.make_async_copy(
        rows_ref, whole_ref.at[pl.ds(pl.multiple_of(me * rows, rows), rows)], local_sem
    )
    local.start()
    pass_copies = []
    for chunk in range(CHUNKS):
        far_copies[chunk].wait_recv()
        block = whole_ref.at[pl.ds(pl.multiple_of(far * rows + chunk * step, step), step)]
        pass_copies.append(remote(block, block, pass_send, pass_recv, chunk, near))
        pass_copies[-1].start()
    for chunk in range(CHUNKS):
        far_copies[chunk].wait_send()
        near_copies[chunk].wait()
    for chunk in range(CHUNKS):
        pass_copies[chunk].wait()
    local.wait()


def gather_tokens(rows, collective_id):
    count, width = rows.shape
    return pl.pallas_call(
        gather_kernel,
        in_specs=[pl.BlockSpec(memory_space=pl.ANY)],
        out_specs=pl.BlockSpec(memory_space=pl.ANY),
        out_shape=jax.ShapeDtypeStruct((4 * count, width), rows.dtype),
        scratch_shapes=[pltpu.SemaphoreType.DMA]
        + [pltpu.SemaphoreType.DMA((CHUNKS,)) for _ in range(6)],
        compiler_params=pltpu.CompilerParams(collective_id=collective_id, has_side_effects=True),
        cost_estimate=pl.CostEstimate(
            flops=2 * count * width, bytes_accessed=count * width, transcendentals=0
        ),
        name="gather_tokens",
    )(rows)


def scatter_kernel(
    partial_ref, sum_ref, first_slot, second_slot, onward, arrived,
    first_send, first_recv, second_send, second_recv, far_send, far_recv,
):
    me, near, far = tp_partners()
    opposite = lax.rem(near + 2, 4)
    rows = sum_ref.shape[0]
    step = rows // CHUNKS

    def remote(source, target, sends, recvs, chunk, peer):
        return pltpu.make_async_remote_copy(
            src_ref=source, dst_ref=target, send_sem=sends.at[chunk], recv_sem=recvs.at[chunk],
            device_id={"tp": peer}, device_id_type=MESH_ID,
        )

    def block(owner, chunk):
        return pl.ds(pl.multiple_of(owner * rows + chunk * step, step), step)

    greet([{"tp": near}, {"tp": far}])
    first_copies = []
    second_copies = []
    far_copies = []
    for chunk in range(CHUNKS):
        first_copies.append(
            remote(
                partial_ref.at[block(opposite, chunk)],
                first_slot.at[pl.ds(chunk * step, step)],
                first_send, first_recv, chunk, near,
            )
        )
        first_copies[-1].start()
    for chunk in range(CHUNKS):
        second_copies.append(
            remote(
                partial_ref.at[block(near, chunk)],
                second_slot.at[pl.ds(chunk * step, step)],
                second_send, second_recv, chunk, near,
            )
        )
        second_copies[-1].start()
    for chunk in range(CHUNKS):
        here = pl.ds(chunk * step, step)
        first_copies[chunk].wait_recv()
        onward[here, :] = (
            partial_ref[block(far, chunk), :].astype(jnp.float32)
            + first_slot[here, :].astype(jnp.float32)
        ).astype(jnp.bfloat16)
        far_copies.append(
            remote(onward.at[here], arrived.at[here], far_send, far_recv, chunk, far)
        )
        far_copies[-1].start()
    for chunk in range(CHUNKS):
        here = pl.ds(chunk * step, step)
        second_copies[chunk].wait_recv()
        far_copies[chunk].wait_recv()
        sum_ref[here, :] = (
            partial_ref[block(me, chunk), :].astype(jnp.float32)
            + second_slot[here, :].astype(jnp.float32)
            + arrived[here, :].astype(jnp.float32)
        )
    for chunk in range(CHUNKS):
        first_copies[chunk].wait_send()
        second_copies[chunk].wait_send()
        far_copies[chunk].wait_send()


def scatter_tokens(partial, collective_id):
    partial = partial.astype(jnp.bfloat16)
    count, width = partial.shape[0] // 4, partial.shape[1]
    return pl.pallas_call(
        scatter_kernel,
        in_specs=[pl.BlockSpec(memory_space=pltpu.VMEM)],
        out_specs=pl.BlockSpec(memory_space=pltpu.VMEM),
        out_shape=jax.ShapeDtypeStruct((count, width), jnp.float32),
        scratch_shapes=[pltpu.VMEM((count, width), jnp.bfloat16) for _ in range(4)]
        + [pltpu.SemaphoreType.DMA((CHUNKS,)) for _ in range(6)],
        compiler_params=pltpu.CompilerParams(
            collective_id=collective_id, has_side_effects=True, vmem_limit_bytes=32 * 1024 * 1024
        ),
        cost_estimate=pl.CostEstimate(
            flops=2 * count * width, bytes_accessed=count * width, transcendentals=0
        ),
        name="scatter_tokens",
    )(partial)


def gains_kernel(
    sizes, part_ref, sum_ref, tp_slots, fsdp_slots, tp_send, tp_recv, fsdp_send, fsdp_recv
):
    stages = (
        ("tp", sizes[0], tp_slots, tp_send, tp_recv),
        ("fsdp", sizes[1], fsdp_slots, fsdp_send, fsdp_recv),
    )
    greet(
        [
            {axis: lax.rem(lax.axis_index(axis) + offset, size)}
            for axis, size, _, _, _ in stages
            for offset in range(1, size)
        ]
    )
    current = part_ref[...]
    for axis, size, slots, sends, recvs in stages:
        me = lax.axis_index(axis)
        slots[me] = current
        copies = []
        for offset in range(1, size):
            copies.append(
                pltpu.make_async_remote_copy(
                    src_ref=slots.at[me], dst_ref=slots.at[me],
                    send_sem=sends.at[offset], recv_sem=recvs.at[offset],
                    device_id={axis: lax.rem(me + offset, size)}, device_id_type=MESH_ID,
                )
            )
            copies[-1].start()
        for copy in copies:
            copy.wait()
        current = slots[0]
        for source in range(1, size):
            current = current + slots[source]
    sum_ref[...] = current


def sum_gains(values, collective_id):
    sizes = (lax.axis_size("tp"), lax.axis_size("fsdp"))
    length = values.shape[0]
    rows = -(-length // 1024) * 8
    part = jnp.pad(values, (0, rows * 128 - length)).reshape(rows, 128)
    total = pl.pallas_call(
        functools.partial(gains_kernel, sizes),
        in_specs=[pl.BlockSpec(memory_space=pltpu.VMEM)],
        out_specs=pl.BlockSpec(memory_space=pltpu.VMEM),
        out_shape=jax.ShapeDtypeStruct((rows, 128), jnp.float32),
        scratch_shapes=[pltpu.VMEM((size, rows, 128), jnp.float32) for size in sizes]
        + [pltpu.SemaphoreType.DMA((size,)) for size in sizes for _ in range(2)],
        compiler_params=pltpu.CompilerParams(collective_id=collective_id, has_side_effects=True),
        name="sum_gains",
    )(part)
    return total.reshape(rows * 128)[:length]


def on_device(
    tokens,
    positions,
    first_gain,
    query_weight,
    key_weight,
    value_weight,
    query_gain,
    key_gain,
    out_weight,
    second_gain,
    gate_weight,
    up_weight,
    down_weight,
    cotangent,
):
    group_rows = positions.shape[0]
    heads_here = query_weight.shape[1] // HEAD_DIM
    pairs_here = key_weight.shape[1] // HEAD_DIM
    share = heads_here // pairs_here
    query_width = query_weight.shape[1]
    key_width = key_weight.shape[1]
    proj_width = query_width + 2 * key_width
    units = gate_weight.shape[1]
    attention_weights = lax.all_gather(
        jnp.concatenate([query_weight, key_weight, value_weight, out_weight.T], axis=1),
        "fsdp", axis=0, tiled=True,
    )
    unit_weights = lax.all_gather(
        jnp.concatenate([gate_weight, up_weight, down_weight.T], axis=1),
        "fsdp", axis=0, tiled=True,
    )
    whole_proj = attention_weights[:, :proj_width]
    whole_out = attention_weights[:, proj_width:]
    whole_gate = unit_weights[:, :units]
    whole_up = unit_weights[:, units : 2 * units]
    whole_down = unit_weights[:, 2 * units :]
    inputs = tokens.astype(jnp.float32)
    unit_one, inverse_one = normalize(inputs)
    normed_one = gather_tokens((unit_one * first_gain).astype(jnp.bfloat16), 1)
    proj = dot_plain(normed_one, whole_proj)
    tables = angle_tables(positions)
    gain_rows = (
        jnp.tile(query_gain, heads_here)[None, :], jnp.tile(key_gain, pairs_here)[None, :]
    )
    rot, context, logsums = attention_forward(proj, tables, gain_rows, pairs_here, share)
    hidden = inputs + scatter_tokens(dot_cols(context, whole_out), 2)
    unit_two, inverse_two = normalize(hidden)
    normed_two = gather_tokens((unit_two * second_gain).astype(jnp.bfloat16), 1)
    grad_result = lax.all_gather(cotangent, "tp", axis=0, tiled=True)
    gate_value = dot_plain(normed_two, whole_gate)
    up_value = dot_plain(normed_two, whole_up)
    sigmoid_gate = jax.nn.sigmoid(gate_value)
    active = gate_value * sigmoid_gate
    mixed_units = (active * up_value).astype(jnp.bfloat16)
    down_partial = dot_cols(mixed_units, whole_down).astype(jnp.bfloat16)
    down_partial, grad_result = lax.optimization_barrier((down_partial, grad_result))
    grad_mixed = dot_plain(grad_result, whole_down)
    grad_gate = (
        grad_mixed * up_value * sigmoid_gate * (1.0 + gate_value * (1.0 - sigmoid_gate))
    ).astype(jnp.bfloat16)
    grad_up = (grad_mixed * active).astype(jnp.bfloat16)
    grad_normed_two = scatter_tokens(
        dot_cols(grad_gate, whole_gate) + dot_cols(grad_up, whole_up), 2
    )
    down_sum = lax.psum_scatter(down_partial, "tp", scatter_dimension=0, tiled=True)
    unit_grads = jnp.concatenate(
        [
            dot_rows(normed_two, grad_gate).astype(jnp.bfloat16),
            dot_rows(normed_two, grad_up).astype(jnp.bfloat16),
            dot_rows(grad_result, mixed_units).astype(jnp.bfloat16),
        ],
        axis=1,
    )
    grad_normed_two, unit_grads, down_sum = lax.optimization_barrier(
        (grad_normed_two, unit_grads, down_sum)
    )
    output = (hidden + down_sum.astype(jnp.float32)).astype(jnp.bfloat16)
    unit_shard = lax.psum_scatter(unit_grads, "fsdp", scatter_dimension=0, tiled=True)
    gain_two = jnp.sum(grad_normed_two * unit_two, axis=0)
    grad_hidden = cotangent.astype(jnp.float32) + norm_back(
        grad_normed_two * second_gain, unit_two, inverse_two
    )
    grad_hidden_all = gather_tokens(grad_hidden.astype(jnp.bfloat16), 1)
    grad_context = dot_plain(grad_hidden_all, whole_out).astype(jnp.bfloat16)
    grad_proj, gain_sums = attention_backward(
        proj, tables, gain_rows, rot, logsums, grad_context, pairs_here, share
    )
    grad_normed_one = scatter_tokens(dot_cols(grad_proj, whole_proj), 2)
    attention_grads = jnp.concatenate(
        [
            dot_rows(normed_one, grad_proj).astype(jnp.bfloat16),
            dot_rows(grad_hidden_all, context).astype(jnp.bfloat16),
        ],
        axis=1,
    )
    attention_grads, unit_shard = lax.optimization_barrier((attention_grads, unit_shard))
    attention_shard = lax.psum_scatter(
        attention_grads, "fsdp", scatter_dimension=0, tiled=True
    ).astype(jnp.float32)
    gain_one = jnp.sum(grad_normed_one * unit_one, axis=0)
    grad_tokens = grad_hidden + norm_back(grad_normed_one * first_gain, unit_one, inverse_one)
    gain_sums = jnp.sum(gain_sums.reshape(-1, 8, query_width + key_width)[:, 0], axis=0)
    gain_query = jnp.sum(gain_sums[:query_width].reshape(heads_here, HEAD_DIM), axis=0)
    gain_key = jnp.sum(gain_sums[query_width:].reshape(pairs_here, HEAD_DIM), axis=0)
    width = first_gain.shape[0]
    gains = sum_gains(jnp.concatenate([gain_one, gain_two, gain_query, gain_key]), 3)
    unit_shard = unit_shard.astype(jnp.float32)
    return (
        output,
        grad_tokens,
        gains[:width],
        attention_shard[:, :query_width],
        attention_shard[:, query_width : query_width + key_width],
        attention_shard[:, query_width + key_width : proj_width],
        gains[2 * width : 2 * width + HEAD_DIM],
        gains[2 * width + HEAD_DIM :],
        attention_shard[:, proj_width:].T,
        gains[width : 2 * width],
        unit_shard[:, :units],
        unit_shard[:, units : 2 * units],
        unit_shard[:, 2 * units :].T,
    )


def solution(mesh):
    return jax.shard_map(
        on_device,
        mesh=mesh,
        in_specs=(
            P(("fsdp", "tp"), None),
            P("fsdp"),
            P(),
            P("fsdp", "tp"),
            P("fsdp", "tp"),
            P("fsdp", "tp"),
            P(),
            P(),
            P("tp", "fsdp"),
            P(),
            P("fsdp", "tp"),
            P("fsdp", "tp"),
            P("tp", "fsdp"),
            P(("fsdp", "tp"), None),
        ),
        out_specs=(
            P(("fsdp", "tp"), None),
            P(("fsdp", "tp"), None),
            P(),
            P("fsdp", "tp"),
            P("fsdp", "tp"),
            P("fsdp", "tp"),
            P(),
            P(),
            P("tp", "fsdp"),
            P(),
            P("fsdp", "tp"),
            P("fsdp", "tp"),
            P("tp", "fsdp"),
        ),
        check_vma=False,
    )
```
